32 devices in a mesh: groups: 2 (over x), cuts: 8 (over z, y), states: 2 (over core).
Axes of the slice: x: 2, y: 2, z: 4, core: 2. Of those that a mesh axis runs over, the one named last changes fastest.
Arguments:
- trial_states: bfloat16 [2, 512, 1024], P('states', ('groups', 'cuts')), parts along dimension 1, may hold values from -6 to 6
- scenario_ids: int32 [2, 512], P('states', ('groups', 'cuts')), parts along dimension 1, may hold values from 0 to 63
- dispatch: bfloat16 [1024, 1024], replicated, may hold values from -0.1875 to 0.1875
- bias: float32 [1024], replicated, may hold values from -3 to 3
- noise: float32 [128, 1024], P('groups'), parts along dimension 0, may hold values from -6 to 6
- cut_slopes: bfloat16 [32768, 1024], P(('groups', 'cuts')), parts along dimension 0, may hold values from -0.1875 to 0.1875
- cut_heights: float32 [32768], P(('groups', 'cuts')), parts along dimension 0, may hold values from -6 to 6
- active_counts: int32 [16], P(('groups', 'cuts')), parts along dimension 0, may hold values from 512 to 2048, as said below
Outputs:
- margins: bfloat16 [32768, 512], P(('groups', 'cuts'), 'states'), parts along dimension 0
The draws below stay inside these ranges and needn't reach their ends.
There are 2 independent parts, one for each index of `groups`. The reference program is written for one: setup_inputs(seed, part) draws one part's arguments, and reference() takes and returns one part's arrays. A program takes and returns all parts, laid end to end along the dimension named above; an argument that names none is the same for every part. Nothing has to cross between parts.
Inputs may be any that keep to these rules, and one draw needn't show every extreme that they name: `scenario_ids`: each is the index of one row of noise. `active_counts`: some shard has all 2048 cuts active in every draw.
All inputs are finite; a program needn't handle non-finite values.
Results may differ from the reference program's by a relative error of at most 0.0029.
Values may be sent and summed in bfloat16 or wider, within the bound.
No kernel may reach another device: no remote copies, remote signals or barrier semaphores. Data moves between devices by JAX's collectives and lax.ppermute only.
A program may use at most 64 MiB of HBM per device.

```python
import jax
import jax.numpy as jnp
from jax import lax

R = 1024
CUT_DEV = 2048
SCEN = 64
CUTS = 16384
S_HALF = 256
S = 512
N_CUTS = 8
N_STATES = 2


def draw_active_counts(key, part):
    key = jax.random.fold_in(key, 11)
    first_key, second_key = jax.random.split(key)
    counts = jax.random.randint(first_key, (N_CUTS,), CUT_DEV // 4, CUT_DEV + 1)
    fullest = jax.random.randint(second_key, (), 0, N_CUTS)
    return jnp.where(jnp.arange(N_CUTS) == fullest, CUT_DEV, counts).astype(jnp.int32)


def place_ends(entries, key, smallest, high):
    dims = entries.shape
    place = [jax.random.randint(jax.random.fold_in(key, axis), (), 0, dims[axis]) for axis in range(len(dims))]
    entries = entries.at[tuple(place)].set(smallest)
    longest = dims.index(max(dims))
    place[longest] = (place[longest] + 1) % dims[longest]
    return entries.at[tuple(place)].set(high)


def level_of(own_key, dims, shards, smallest, high):
    gain, own = 1.0, jax.random.fold_in(own_key, 6)
    for dim, blocks in shards:
        steps = jnp.exp(jax.random.uniform(jax.random.fold_in(own, dim), (blocks,), jnp.float32, smallest / len(shards), high / len(shards)))
        gain = gain * jnp.repeat(steps, dims[dim] // blocks).reshape([-1 if axis == dim else 1 for axis in range(len(dims))])
    return gain


def bell_draw(stream_key, dims, deviation, most, cuts=(), kind=jnp.bfloat16):
    array = deviation * jax.random.normal(stream_key, dims, jnp.float32)
    if cuts:
        array = array * level_of(stream_key, dims, cuts, -0.22, 0.18)
    return jnp.clip(array, -most, most).astype(kind)


def setup_inputs(seed: int = 0, part: int = 0) -> dict:
    arg_keys = jax.random.split(jax.random.key(seed), 9)
    part_keys = jax.random.split(jax.random.fold_in(arg_keys[8], part), 9)
    trial_states = bell_draw(part_keys[0], (N_STATES, S_HALF, R), 1.0, 6.0, ((0, 2), (1, 8)))
    scenario_ids = place_ends(jax.random.randint(part_keys[1], (N_STATES, S_HALF), 0, SCEN), jax.random.fold_in(part_keys[1], 1), 0, SCEN - 1).astype(jnp.int32)
    dispatch = bell_draw(arg_keys[2], (R, R), R ** -0.5, 0.1875)
    bias = bell_draw(arg_keys[3], (R,), 0.5, 3.0, (), jnp.float32)
    noise = bell_draw(part_keys[4], (SCEN, R), 1.0, 6.0, (), jnp.float32)
    cut_slopes = bell_draw(part_keys[5], (CUTS, R), R ** -0.5, 0.1875, ((0, 8),))
    cut_heights = bell_draw(part_keys[6], (CUTS,), 1.0, 6.0, ((0, 8),), jnp.float32)
    active_counts = draw_active_counts(jax.random.fold_in(jax.random.fold_in(arg_keys[8], part), 71), part)
    return {"trial_states": trial_states, "scenario_ids": scenario_ids, "dispatch": dispatch, "bias": bias, "noise": noise, "cut_slopes": cut_slopes, "cut_heights": cut_heights, "active_counts": active_counts}


NEG = -1.0e30


def top_two(cands):
    first = jnp.max(cands, axis=0)
    ties = jnp.sum((cands == first[None, :]).astype(jnp.int32), axis=0)
    below = jnp.max(jnp.where(cands < first[None, :], cands, NEG), axis=0)
    return first, jnp.where(ties >= 2, first, below)


def reference(trial_states, scenario_ids, dispatch, bias, noise, cut_slopes, cut_heights, active_counts):
    trials = trial_states.reshape(S, R)
    picks = scenario_ids.reshape(S)
    flow = jnp.dot(trials, dispatch, preferred_element_type=jnp.float32) + bias[None, :] + noise[picks]
    next_state = jnp.maximum(flow, 0.0).astype(jnp.bfloat16)
    slope_blocks = cut_slopes.reshape(N_CUTS, CUT_DEV, R)
    height_blocks = cut_heights.reshape(N_CUTS, CUT_DEV)
    rows = jnp.arange(CUT_DEV, dtype=jnp.int32)

    def block_values(inputs):
        slopes, heights, count = inputs
        values = jnp.dot(slopes, next_state.T, preferred_element_type=jnp.float32) + heights[:, None]
        active = (rows < count)[:, None]
        first, second = top_two(jnp.where(active, values, NEG))
        return values, first, second

    values, firsts, seconds = lax.map(block_values, (slope_blocks, height_blocks, active_counts))
    top1, top2 = top_two(jnp.concatenate([firsts, seconds], axis=0))
    active = (rows[None, :] < active_counts[:, None])[:, :, None]
    other = jnp.where(values >= top1[None, None, :], top2[None, None, :], top1[None, None, :])
    margins = jnp.where(active, values - other, 0.0).astype(jnp.bfloat16)
    return margins.reshape(CUTS, S)
```

```python
import functools

import jax
import jax.numpy as jnp
from jax import lax
from jax.experimental import pallas as pl
from jax.experimental.pallas import tpu as pltpu
from jax.sharding import PartitionSpec as P

NEG = -1e30
MIB = 1024 * 1024
LANES = 128
LAST = (3, 2, 1)
VMEM = pl.BlockSpec(memory_space=pltpu.VMEM)
HBM = pl.BlockSpec(memory_space=pltpu.HBM)
SMEM = pl.BlockSpec(memory_space=pltpu.SMEM)


def swap(array, step):
    n = lax.axis_size("cuts")
    return lax.ppermute(array, "cuts", [(i, i ^ step) for i in range(n)])


def early_steps(n):
    steps, step = [], n // 2
    while step >= 4:
        steps.append(step)
        step //= 2
    return steps


def merge(left, right):
    high, low = jnp.maximum(left[0:1], right[0:1]), jnp.minimum(left[0:1], right[0:1])
    return jnp.concatenate([high, jnp.maximum(low, jnp.maximum(left[1:2], right[1:2]))], axis=0)


def split_in_three(values):
    high = values.astype(jnp.bfloat16)
    rest = values - high.astype(jnp.float32)
    mid = rest.astype(jnp.bfloat16)
    return high, mid, (rest - mid.astype(jnp.float32)).astype(jnp.bfloat16)


def roll(trials, ids, dispatch_ref, bias, noise_ref):
    scenarios = lax.broadcasted_iota(jnp.int32, (noise_ref.shape[0] // 3, ids.shape[1]), 0)
    chosen = jnp.where(scenarios == ids, 1.0, 0.0)
    chosen = jnp.concatenate([chosen] * 3, axis=0).astype(jnp.bfloat16)
    inflow = lax.dot_general(
        chosen, noise_ref[...], (((0,), (0,)), ((), ())), preferred_element_type=jnp.float32
    )
    flow = jnp.dot(trials, dispatch_ref[...], preferred_element_type=jnp.float32)
    return jnp.maximum(flow + bias + inflow, 0.0).astype(jnp.bfloat16)


def stage_kernel(
    trials_hbm, ids_hbm, dispatch_hbm, bias_hbm, noise_hbm, heights_hbm, slopes_hbm,
    own_ref, dispatch_ref, bias_ref, noise3_ref, columns_ref, slopes_ref,
    trials_ref, ids_ref, noise_ref, heights_ref, sems,
):
    pairs = (
        (noise_hbm, noise_ref),
        (trials_hbm, trials_ref),
        (ids_hbm, ids_ref),
        (bias_hbm, bias_ref),
        (heights_hbm, heights_ref),
        (dispatch_hbm, dispatch_ref),
        (slopes_hbm, slopes_ref),
    )
    copies = [pltpu.make_async_copy(src, dst, sems.at[i]) for i, (src, dst) in enumerate(pairs)]
    for copy in copies:
        copy.start()
    copies[0].wait()
    scenarios = noise_ref.shape[0]
    for i, term in enumerate(split_in_three(noise_ref[...])):
        noise3_ref[i * scenarios : (i + 1) * scenarios, :] = term
    for copy in copies[1:5]:
        copy.wait()
    for i in range(heights_ref.shape[0]):
        column = jnp.broadcast_to(heights_ref[i : i + 1, :], (LANES, LANES)).T
        columns_ref[i * LANES : (i + 1) * LANES, :] = column
    copies[5].wait()
    own_ref[...] = roll(trials_ref[...], ids_ref[...], dispatch_ref, bias_ref[...], noise3_ref)
    copies[6].wait()


def roll_kernel(own_ref, other_ref, ids_ref, dispatch_ref, bias_ref, noise3_ref, out_ref):
    rows = own_ref.shape[0]
    out_ref[0:rows, :] = own_ref[...]
    out_ref[rows:, :] = roll(other_ref[...], ids_ref[...], dispatch_ref, bias_ref[...], noise3_ref)


def sublane_top_two(first, second):
    size = first.shape[0]
    while size > 1:
        half = size // 2
        a1, b1, a2, b2 = first[:half], first[half:size], second[:half], second[half:size]
        first, second = jnp.maximum(a1, b1), jnp.maximum(jnp.minimum(a1, b1), jnp.maximum(a2, b2))
        size = half
    return first, second


def values_kernel(offsets, block, *refs):
    counts_ref, slopes_ref, heights_ref = refs[:3]
    pieces, (values_ref, tops_ref, states_ref) = refs[3:-3], refs[-3:]
    me = lax.axis_index("cuts")
    held = len(offsets) // len(pieces)
    rows = pieces[0].shape[0] // held
    for i, offset in enumerate(offsets):
        piece, slot = pieces[i // held], i % held
        start = pl.multiple_of((me ^ offset) * rows, rows)
        states_ref[pl.ds(start, rows), :] = piece[slot * rows : (slot + 1) * rows, :]
    count = counts_ref[0]
    cuts, chunk = slopes_ref.shape[0], min(512, slopes_ref.shape[0])

    def on_block(column):
        states = states_ref[pl.ds(column, block), :]
        first = jnp.full((8, block), NEG, jnp.float32)
        second = first
        for start in range(0, cuts, chunk):
            here = lax.dot_general(
                slopes_ref[start : start + chunk, :],
                states,
                (((1,), (1,)), ((), ())),
                preferred_element_type=jnp.float32,
            )
            heights = heights_ref[start : start + chunk, :]
            here = here + jnp.concatenate([heights] * (block // LANES), axis=1)
            values_ref[start : start + chunk, pl.ds(column, block)] = here
            row = lax.broadcasted_iota(jnp.int32, (chunk, block), 0) + start
            here = jnp.where(row < count, here, NEG)
            for sub in range(0, chunk, 8):
                v = here[sub : sub + 8]
                second = jnp.maximum(second, jnp.minimum(first, v))
                first = jnp.maximum(first, v)
        first, second = sublane_top_two(first, second)
        tops_ref[0:1, pl.ds(column, block)] = first
        tops_ref[1:2, pl.ds(column, block)] = second

    blocks = states_ref.shape[0] // block
    if blocks == 1:
        on_block(0)
    else:

        @pl.loop(0, blocks)
        def _(b):
            on_block(pl.multiple_of(b * block, block))


def margins_kernel(chunk, counts_ref, values_ref, *refs):
    tops, (out_ref, held_ref, sems) = refs[:-3], refs[-3:]
    total = tops[0][...]
    for other in tops[1:]:
        total = merge(total, other[...])
    top1, top2 = total[0:1], total[1:2]
    count = counts_ref[0]
    cuts = values_ref.shape[0]
    copies = []
    for i in range(cuts // chunk):
        rows = slice(i * chunk, (i + 1) * chunk)
        values = values_ref[rows, :]
        row = lax.broadcasted_iota(jnp.int32, values.shape, 0) + i * chunk
        margin = values - jnp.where(values >= top1, top2, top1)
        held_ref[rows, :] = jnp.where(row < count, margin, 0.0).astype(jnp.bfloat16)
        copy = pltpu.make_async_copy(held_ref.at[rows], out_ref.at[rows], sems.at[i])
        copy.start()
        copies.append(copy)
    for copy in copies:
        copy.wait()


def on_device(
    trial_states, scenario_ids, dispatch, bias, noise, cut_slopes, cut_heights, active_counts
):
    n = lax.axis_size("cuts")
    steps = early_steps(n)
    trials = trial_states[0]
    rows, width = trials.shape
    half, cuts = rows * n, cut_slopes.shape[0]

    other, other_ids = swap(trials, steps[0]), swap(scenario_ids, steps[0])
    scenarios = noise.shape[0]
    heights = cut_heights.reshape(cuts // LANES, LANES)
    sources = (trials, scenario_ids, dispatch, bias[None, :], noise, heights, cut_slopes)
    own, dispatch, bias, noise3, heights, slopes = pl.pallas_call(
        stage_kernel,
        out_shape=(
            jax.ShapeDtypeStruct((rows, width), jnp.bfloat16),
            jax.ShapeDtypeStruct(dispatch.shape, dispatch.dtype),
            jax.ShapeDtypeStruct((1, width), jnp.float32),
            jax.ShapeDtypeStruct((3 * scenarios, width), jnp.bfloat16),
            jax.ShapeDtypeStruct((cuts, LANES), jnp.float32),
            jax.ShapeDtypeStruct(cut_slopes.shape, cut_slopes.dtype),
        ),
        in_specs=[HBM] * 7,
        out_specs=(VMEM,) * 6,
        scratch_shapes=[
            pltpu.VMEM((rows, width), jnp.bfloat16),
            pltpu.VMEM(scenario_ids.shape, jnp.int32),
            pltpu.VMEM(noise.shape, jnp.float32),
            pltpu.VMEM((cuts // LANES, LANES), jnp.float32),
            pltpu.SemaphoreType.DMA((7,)),
        ],
        compiler_params=pltpu.CompilerParams(vmem_limit_bytes=16 * MIB),
        cost_estimate=pl.CostEstimate(
            flops=2 * rows * width * width,
            bytes_accessed=2 * width * (width + cuts),
            transcendentals=0,
        ),
        name="stage",
    )(*(pltpu.with_memory_space_constraint(array, pltpu.HBM) for array in sources))
    held = pl.pallas_call(
        roll_kernel,
        out_shape=jax.ShapeDtypeStruct((2 * rows, width), jnp.bfloat16),
        in_specs=[VMEM] * 6,
        out_specs=VMEM,
        compiler_params=pltpu.CompilerParams(vmem_limit_bytes=16 * MIB),
        cost_estimate=pl.CostEstimate(
            flops=2 * rows * width * width, bytes_accessed=2 * width * width, transcendentals=0
        ),
        name="roll_forward",
    )(own, other, other_ids, dispatch, bias, noise3)
    offsets = [0, steps[0]]
    for step in steps[1:]:
        held = jnp.concatenate([held, swap(held, step)], axis=0)
        offsets = offsets + [offset ^ step for offset in offsets]
    pieces = [held] + [swap(held, step) for step in LAST]
    offsets = [offset ^ step for step in (0, *LAST) for offset in offsets]

    values, tops = pl.pallas_call(
        functools.partial(values_kernel, offsets, min(256, half)),
        out_shape=(
            jax.ShapeDtypeStruct((cuts, half), jnp.float32),
            jax.ShapeDtypeStruct((2, half), jnp.float32),
        ),
        in_specs=[SMEM] + [VMEM] * (2 + len(pieces)),
        out_specs=(VMEM, VMEM),
        scratch_shapes=[pltpu.VMEM((half, width), jnp.bfloat16)],
        compiler_params=pltpu.CompilerParams(vmem_limit_bytes=32 * MIB),
        cost_estimate=pl.CostEstimate(
            flops=2 * cuts * half * width, bytes_accessed=2 * cuts * width, transcendentals=0
        ),
        name="cut_values",
    )(active_counts, slopes, heights, *pieces)

    for step in steps:
        tops = merge(tops, swap(tops, step))
    sets = [tops] + [swap(tops, step) for step in LAST]

    chunk = min(256, cuts)
    return pl.pallas_call(
        functools.partial(margins_kernel, chunk),
        out_shape=jax.ShapeDtypeStruct((cuts, half), jnp.bfloat16),
        in_specs=[SMEM] + [VMEM] * (1 + len(sets)),
        out_specs=pl.BlockSpec(memory_space=pl.ANY),
        scratch_shapes=[
            pltpu.VMEM((cuts, half), jnp.bfloat16),
            pltpu.SemaphoreType.DMA((cuts // chunk,)),
        ],
        compiler_params=pltpu.CompilerParams(vmem_limit_bytes=16 * MIB),
        cost_estimate=pl.CostEstimate(
            flops=4 * cuts * half, bytes_accessed=2 * cuts * half, transcendentals=0
        ),
        name="margins",
    )(active_counts, values, *sets)


def solution(mesh):
    placed = (
        P("states", ("groups", "cuts"), None),
        P("states", ("groups", "cuts")),
        P(),
        P(),
        P("groups", None),
        P(("groups", "cuts"), None),
        P(("groups", "cuts")),
        P(("groups", "cuts")),
    )
    return jax.shard_map(
        on_device,
        mesh=mesh,
        in_specs=placed,
        out_specs=P(("groups", "cuts"), "states"),
        check_vma=False,
    )
```

```python
import functools

import jax
import jax.numpy as jnp
from jax import lax
from jax.experimental import pallas as pl
from jax.experimental.pallas import tpu as pltpu
from jax.sharding import PartitionSpec as P

NEG = -1e30
MIB = 1024 * 1024
LANES = 128
NEAR_STATES = (3, 1, 2)
EARLY_TOPS, LATE_TOPS = ((1, 1), (0, 1)), (3, 2)
VMEM = pl.BlockSpec(memory_space=pltpu.VMEM)
HBM = pl.BlockSpec(memory_space=pltpu.HBM)
SMEM = pl.BlockSpec(memory_space=pltpu.SMEM)


def swap(array, step):
    n = lax.axis_size("cuts")
    return lax.ppermute(array, "cuts", [(i, i ^ step) for i in range(n)])


def early_steps(n):
    steps, step = [], n // 2
    while step >= 4:
        steps.append(step)
        step //= 2
    return steps


def merge(left, right):
    high, low = jnp.maximum(left[0:1], right[0:1]), jnp.minimum(left[0:1], right[0:1])
    return jnp.concatenate([high, jnp.maximum(low, jnp.maximum(left[1:2], right[1:2]))], axis=0)


def split_in_three(values):
    high = values.astype(jnp.bfloat16)
    rest = values - high.astype(jnp.float32)
    mid = rest.astype(jnp.bfloat16)
    return high, mid, (rest - mid.astype(jnp.float32)).astype(jnp.bfloat16)


def inflow_of(ids, noise_ref):
    scenarios = lax.broadcasted_iota(jnp.int32, (noise_ref.shape[0] // 3, ids.shape[1]), 0)
    chosen = jnp.where(scenarios == ids, 1.0, 0.0)
    chosen = jnp.concatenate([chosen] * 3, axis=0).astype(jnp.bfloat16)
    return lax.dot_general(
        chosen, noise_ref[...], (((0,), (0,)), ((), ())), preferred_element_type=jnp.float32
    )


def flow_of(trials, dispatch_ref, bias):
    return jnp.dot(trials, dispatch_ref[...], preferred_element_type=jnp.float32) + bias


def next_of(flow, inflow):
    return jnp.maximum(flow + inflow, 0.0).astype(jnp.bfloat16)


def stage_kernel(
    trials_hbm, ids_hbm, dispatch_hbm, bias_hbm, noise_hbm, heights_hbm, slopes_hbm,
    own_ref, dispatch_ref, bias_ref, noise3_ref, columns_ref, slopes_ref,
    trials_ref, ids_ref, noise_ref, heights_ref, sems,
):
    pairs = (
        (noise_hbm, noise_ref),
        (trials_hbm, trials_ref),
        (ids_hbm, ids_ref),
        (bias_hbm, bias_ref),
        (heights_hbm, heights_ref),
        (dispatch_hbm, dispatch_ref),
        (slopes_hbm, slopes_ref),
    )
    copies = [pltpu.make_async_copy(src, dst, sems.at[i]) for i, (src, dst) in enumerate(pairs)]
    for copy in copies:
        copy.start()
    copies[0].wait()
    scenarios = noise_ref.shape[0]
    for i, term in enumerate(split_in_three(noise_ref[...])):
        noise3_ref[i * scenarios : (i + 1) * scenarios, :] = term
    for copy in copies[1:5]:
        copy.wait()
    for i in range(heights_ref.shape[0]):
        column = jnp.broadcast_to(heights_ref[i : i + 1, :], (LANES, LANES)).T
        columns_ref[i * LANES : (i + 1) * LANES, :] = column
    copies[5].wait()
    flow = flow_of(trials_ref[...], dispatch_ref, bias_ref[...])
    own_ref[...] = next_of(flow, inflow_of(ids_ref[...], noise3_ref))
    copies[6].wait()


def flow_kernel(other_ref, dispatch_ref, bias_ref, flow_ref):
    flow_ref[...] = flow_of(other_ref[...], dispatch_ref, bias_ref[...])


def join_kernel(own_ref, flow_ref, ids_ref, noise3_ref, out_ref):
    rows = own_ref.shape[0]
    out_ref[0:rows, :] = own_ref[...]
    out_ref[rows:, :] = next_of(flow_ref[...], inflow_of(ids_ref[...], noise3_ref))


def sublane_top_two(first, second):
    size = first.shape[0]
    while size > 1:
        half = size // 2
        a1, b1, a2, b2 = first[:half], first[half:size], second[:half], second[half:size]
        first, second = jnp.maximum(a1, b1), jnp.maximum(jnp.minimum(a1, b1), jnp.maximum(a2, b2))
        size = half
    return first, second


def values_kernel(offsets, block, *refs):
    counts_ref, slopes_ref, heights_ref = refs[:3]
    pieces, (values_ref, tops_ref, states_ref) = refs[3:-3], refs[-3:]
    me = lax.axis_index("cuts")
    held = len(offsets) // len(pieces)
    rows = pieces[0].shape[0] // held
    for i, offset in enumerate(offsets):
        piece, slot = pieces[i // held], i % held
        start = pl.multiple_of((me ^ offset) * rows, rows)
        states_ref[pl.ds(start, rows), :] = piece[slot * rows : (slot + 1) * rows, :]
    cuts, chunk = slopes_ref.shape[0], min(256, slopes_ref.shape[0])

    def on_block(column):
        states = states_ref[pl.ds(column, block), :]
        first = jnp.full((8, block), NEG, jnp.float32)
        second = first
        for start in range(0, cuts, chunk):
            here = lax.dot_general(
                slopes_ref[start : start + chunk, :],
                states,
                (((1,), (1,)), ((), ())),
                preferred_element_type=jnp.float32,
            )
            heights = heights_ref[start : start + chunk, :]
            here = here + jnp.concatenate([heights] * (block // LANES), axis=1)
            values_ref[start : start + chunk, pl.ds(column, block)] = here
            row = lax.broadcasted_iota(jnp.int32, (chunk, block), 0) + start
            here = jnp.where(row < counts_ref[0], here, NEG)
            for sub in range(0, chunk, 8):
                v = here[sub : sub + 8]
                second = jnp.maximum(second, jnp.minimum(first, v))
                first = jnp.maximum(first, v)
        first, second = sublane_top_two(first, second)
        tops_ref[0:1, pl.ds(column, block)] = first
        tops_ref[1:2, pl.ds(column, block)] = second

    blocks = states_ref.shape[0] // block
    if blocks == 1:
        on_block(0)
    else:

        @pl.loop(0, blocks)
        def _(b):
            on_block(pl.multiple_of(b * block, block))


def margins_kernel(chunk, counts_ref, values_ref, *refs):
    tops, (out_ref, held_ref, sems) = refs[:-3], refs[-3:]
    total = tops[0][...]
    for other in tops[1:]:
        total = merge(total, other[...])
    top1, top2 = total[0:1], total[1:2]
    count = counts_ref[0]
    cuts = values_ref.shape[0]
    copies = []
    for i in range(cuts // chunk):
        rows = slice(i * chunk, (i + 1) * chunk)
        values = values_ref[rows, :]
        row = lax.broadcasted_iota(jnp.int32, values.shape, 0) + i * chunk
        margin = values - jnp.where(values >= top1, top2, top1)
        held_ref[rows, :] = jnp.where(row < count, margin, 0.0).astype(jnp.bfloat16)
        copy = pltpu.make_async_copy(held_ref.at[rows], out_ref.at[rows], sems.at[i])
        copy.start()
        copies.append(copy)
    for copy in copies:
        copy.wait()


def on_device(
    trial_states, scenario_ids, dispatch, bias, noise, cut_slopes, cut_heights, active_counts
):
    n = lax.axis_size("cuts")
    steps = early_steps(n)
    trials = trial_states[0]
    rows, width = trials.shape
    half, cuts = rows * n, cut_slopes.shape[0]

    other, other_ids = swap(trials, steps[0]), swap(scenario_ids, steps[0])
    scenarios = noise.shape[0]
    heights = cut_heights.reshape(cuts // LANES, LANES)
    sources = (trials, scenario_ids, dispatch, bias[None, :], noise, heights, cut_slopes)
    own, dispatch, bias, noise3, heights, slopes = pl.pallas_call(
        stage_kernel,
        out_shape=(
            jax.ShapeDtypeStruct((rows, width), jnp.bfloat16),
            jax.ShapeDtypeStruct(dispatch.shape, dispatch.dtype),
            jax.ShapeDtypeStruct((1, width), jnp.float32),
            jax.ShapeDtypeStruct((3 * scenarios, width), jnp.bfloat16),
            jax.ShapeDtypeStruct((cuts, LANES), jnp.float32),
            jax.ShapeDtypeStruct(cut_slopes.shape, cut_slopes.dtype),
        ),
        in_specs=[HBM] * 7,
        out_specs=(VMEM,) * 6,
        scratch_shapes=[
            pltpu.VMEM((rows, width), jnp.bfloat16),
            pltpu.VMEM(scenario_ids.shape, jnp.int32),
            pltpu.VMEM(noise.shape, jnp.float32),
            pltpu.VMEM((cuts // LANES, LANES), jnp.float32),
            pltpu.SemaphoreType.DMA((7,)),
        ],
        compiler_params=pltpu.CompilerParams(vmem_limit_bytes=16 * MIB),
        cost_estimate=pl.CostEstimate(
            flops=2 * rows * width * width,
            bytes_accessed=2 * width * (width + cuts),
            transcendentals=0,
        ),
        name="stage",
    )(*(pltpu.with_memory_space_constraint(array, pltpu.HBM) for array in sources))
    flow = pl.pallas_call(
        flow_kernel,
        out_shape=jax.ShapeDtypeStruct((rows, width), jnp.float32),
        in_specs=[VMEM] * 3,
        out_specs=VMEM,
        compiler_params=pltpu.CompilerParams(vmem_limit_bytes=8 * MIB),
        cost_estimate=pl.CostEstimate(
            flops=2 * rows * width * width, bytes_accessed=2 * width * width, transcendentals=0
        ),
        name="flow",
    )(other, dispatch, bias)
    held = pl.pallas_call(
        join_kernel,
        out_shape=jax.ShapeDtypeStruct((2 * rows, width), jnp.bfloat16),
        in_specs=[VMEM] * 4,
        out_specs=VMEM,
        compiler_params=pltpu.CompilerParams(vmem_limit_bytes=8 * MIB),
        cost_estimate=pl.CostEstimate(
            flops=6 * rows * scenarios * width, bytes_accessed=8 * rows * width, transcendentals=0
        ),
        name="inflow_join",
    )(own, flow, other_ids, noise3)
    offsets = [0, steps[0]]
    for step in steps[1:]:
        held = jnp.concatenate([held, swap(held, step)], axis=0)
        offsets = offsets + [offset ^ step for offset in offsets]
    pieces = [held] + [swap(held, step) for step in NEAR_STATES]
    offsets = [offset ^ step for step in (0, *NEAR_STATES) for offset in offsets]

    values, tops = pl.pallas_call(
        functools.partial(values_kernel, offsets, min(256, half)),
        out_shape=(
            jax.ShapeDtypeStruct((cuts, half), jnp.float32),
            jax.ShapeDtypeStruct((2, half), jnp.float32),
        ),
        in_specs=[SMEM] + [VMEM] * (2 + len(pieces)),
        out_specs=(VMEM, VMEM),
        scratch_shapes=[pltpu.VMEM((half, width), jnp.bfloat16)],
        compiler_params=pltpu.CompilerParams(vmem_limit_bytes=32 * MIB),
        cost_estimate=pl.CostEstimate(
            flops=2 * cuts * half * width, bytes_accessed=2 * cuts * width, transcendentals=0
        ),
        name="cut_values",
    )(active_counts, slopes, heights, *pieces)

    for step in steps[:-1]:
        tops = merge(tops, swap(tops, step))
    far = steps[-1]
    sets = [swap(tops, far * bit ^ near) for bit, near in ((1, 0), *EARLY_TOPS)]
    tops = merge(tops, sets[0])
    sets = [tops, *sets[1:], *(swap(tops, step) for step in LATE_TOPS)]

    chunk = min(256, cuts)
    return pl.pallas_call(
        functools.partial(margins_kernel, chunk),
        out_shape=jax.ShapeDtypeStruct((cuts, half), jnp.bfloat16),
        in_specs=[SMEM] + [VMEM] * (1 + len(sets)),
        out_specs=pl.BlockSpec(memory_space=pl.ANY),
        scratch_shapes=[
            pltpu.VMEM((cuts, half), jnp.bfloat16),
            pltpu.SemaphoreType.DMA((cuts // chunk,)),
        ],
        compiler_params=pltpu.CompilerParams(vmem_limit_bytes=16 * MIB),
        cost_estimate=pl.CostEstimate(
            flops=4 * cuts * half, bytes_accessed=2 * cuts * half, transcendentals=0
        ),
        name="margins",
    )(active_counts, values, *sets)


def solution(mesh):
    placed = (
        P("states", ("groups", "cuts"), None),
        P("states", ("groups", "cuts")),
        P(),
        P(),
        P("groups", None),
        P(("groups", "cuts"), None),
        P(("groups", "cuts")),
        P(("groups", "cuts")),
    )
    return jax.shard_map(
        on_device,
        mesh=mesh,
        in_specs=placed,
        out_specs=P(("groups", "cuts"), "states"),
        check_vma=False,
    )
```

```python
import functools

import jax
import jax.numpy as jnp
from jax import lax
from jax.experimental import pallas as pl
from jax.experimental.pallas import tpu as pltpu
from jax.sharding import PartitionSpec as P

NEG = -1e30
MIB = 1024 * 1024
LANES = 128
NEAR_STATES = (3, 1, 2)
EARLY_TOPS, LATE_TOPS = ((0, 1), (1, 1)), (3, 2)
VMEM = pl.BlockSpec(memory_space=pltpu.VMEM)
HBM = pl.BlockSpec(memory_space=pltpu.HBM)
SMEM = pl.BlockSpec(memory_space=pltpu.SMEM)


def swap(array, step):
    n = lax.axis_size("cuts")
    return lax.ppermute(array, "cuts", [(i, i ^ step) for i in range(n)])


def early_steps(n):
    steps, step = [], n // 2
    while step >= 4:
        steps.append(step)
        step //= 2
    return steps


def merge(left, right):
    high, low = jnp.maximum(left[0:1], right[0:1]), jnp.minimum(left[0:1], right[0:1])
    return jnp.concatenate([high, jnp.maximum(low, jnp.maximum(left[1:2], right[1:2]))], axis=0)


def split_in_three(values):
    high = values.astype(jnp.bfloat16)
    rest = values - high.astype(jnp.float32)
    mid = rest.astype(jnp.bfloat16)
    return high, mid, (rest - mid.astype(jnp.float32)).astype(jnp.bfloat16)


def inflow_of(ids, noise_ref):
    scenarios = lax.broadcasted_iota(jnp.int32, (noise_ref.shape[0] // 3, ids.shape[1]), 0)
    chosen = jnp.where(scenarios == ids, 1.0, 0.0)
    chosen = jnp.concatenate([chosen] * 3, axis=0).astype(jnp.bfloat16)
    return lax.dot_general(
        chosen, noise_ref[...], (((0,), (0,)), ((), ())), preferred_element_type=jnp.float32
    )


def flow_of(trials, dispatch_ref, bias):
    return jnp.dot(trials, dispatch_ref[...], preferred_element_type=jnp.float32) + bias


def next_of(flow, inflow):
    return jnp.maximum(flow + inflow, 0.0).astype(jnp.bfloat16)


def stage_kernel(
    trials_hbm, ids_hbm, dispatch_hbm, bias_hbm, noise_hbm, heights_hbm, slopes_hbm,
    own_ref, dispatch_ref, bias_ref, noise3_ref, columns_ref, slopes_ref,
    trials_ref, ids_ref, noise_ref, heights_ref, sems,
):
    pairs = (
        (noise_hbm, noise_ref),
        (trials_hbm, trials_ref),
        (ids_hbm, ids_ref),
        (bias_hbm, bias_ref),
        (heights_hbm, heights_ref),
        (dispatch_hbm, dispatch_ref),
        (slopes_hbm, slopes_ref),
    )
    copies = [pltpu.make_async_copy(src, dst, sems.at[i]) for i, (src, dst) in enumerate(pairs)]
    for copy in copies:
        copy.start()
    copies[0].wait()
    scenarios = noise_ref.shape[0]
    for i, term in enumerate(split_in_three(noise_ref[...])):
        noise3_ref[i * scenarios : (i + 1) * scenarios, :] = term
    for copy in copies[1:5]:
        copy.wait()
    for i in range(heights_ref.shape[0]):
        column = jnp.broadcast_to(heights_ref[i : i + 1, :], (LANES, LANES)).T
        columns_ref[i * LANES : (i + 1) * LANES, :] = column
    copies[5].wait()
    flow = flow_of(trials_ref[...], dispatch_ref, bias_ref[...])
    own_ref[...] = next_of(flow, inflow_of(ids_ref[...], noise3_ref))
    copies[6].wait()


def flow_kernel(other_ref, dispatch_ref, bias_ref, flow_ref):
    flow_ref[...] = flow_of(other_ref[...], dispatch_ref, bias_ref[...])


def join_kernel(own_ref, flow_ref, ids_ref, noise3_ref, out_ref):
    rows = own_ref.shape[0]
    out_ref[0:rows, :] = own_ref[...]
    out_ref[rows:, :] = next_of(flow_ref[...], inflow_of(ids_ref[...], noise3_ref))


def sublane_top_two(first, second):
    size = first.shape[0]
    while size > 1:
        half = size // 2
        a1, b1, a2, b2 = first[:half], first[half:size], second[:half], second[half:size]
        first, second = jnp.maximum(a1, b1), jnp.maximum(jnp.minimum(a1, b1), jnp.maximum(a2, b2))
        size = half
    return first, second


def values_kernel(offsets, block, *refs):
    counts_ref, slopes_ref, heights_ref = refs[:3]
    pieces, (values_ref, tops_ref, states_ref) = refs[3:-3], refs[-3:]
    me = lax.axis_index("cuts")
    held = len(offsets) // len(pieces)
    rows = pieces[0].shape[0] // held
    for i, offset in enumerate(offsets):
        piece, slot = pieces[i // held], i % held
        start = pl.multiple_of((me ^ offset) * rows, rows)
        states_ref[pl.ds(start, rows), :] = piece[slot * rows : (slot + 1) * rows, :]
    cuts, chunk = slopes_ref.shape[0], min(256, slopes_ref.shape[0])

    def on_block(column):
        states = states_ref[pl.ds(column, block), :]
        first = jnp.full((8, block), NEG, jnp.float32)
        second = first
        for start in range(0, cuts, chunk):
            here = lax.dot_general(
                slopes_ref[start : start + chunk, :],
                states,
                (((1,), (1,)), ((), ())),
                preferred_element_type=jnp.float32,
            )
            row = lax.broadcasted_iota(jnp.int32, (chunk, LANES), 0) + start
            heights = jnp.where(row < counts_ref[0], heights_ref[start : start + chunk, :], NEG)
            here = here + jnp.concatenate([heights] * (block // LANES), axis=1)
            values_ref[start : start + chunk, pl.ds(column, block)] = here
            for sub in range(0, chunk, 8):
                v = here[sub : sub + 8]
                second = jnp.maximum(second, jnp.minimum(first, v))
                first = jnp.maximum(first, v)
        first, second = sublane_top_two(first, second)
        tops_ref[0:1, pl.ds(column, block)] = first
        tops_ref[1:2, pl.ds(column, block)] = second

    blocks = states_ref.shape[0] // block
    if blocks == 1:
        on_block(0)
    else:

        @pl.loop(0, blocks)
        def _(b):
            on_block(pl.multiple_of(b * block, block))


def margins_kernel(chunk, counts_ref, values_ref, *refs):
    tops, (out_ref, held_ref, sems) = refs[:-3], refs[-3:]
    total = tops[0][...]
    for other in tops[1:]:
        total = merge(total, other[...])
    top1, top2 = total[0:1], total[1:2]
    count = counts_ref[0]
    cuts = values_ref.shape[0]
    copies = []
    for i in range(cuts // chunk):
        rows = slice(i * chunk, (i + 1) * chunk)
        values = values_ref[rows, :]
        row = lax.broadcasted_iota(jnp.int32, values.shape, 0) + i * chunk
        margin = values - jnp.where(values >= top1, top2, top1)
        held_ref[rows, :] = jnp.where(row < count, margin, 0.0).astype(jnp.bfloat16)
        copy = pltpu.make_async_copy(held_ref.at[rows], out_ref.at[rows], sems.at[i])
        copy.start()
        copies.append(copy)
    for copy in copies:
        copy.wait()


def on_device(
    trial_states, scenario_ids, dispatch, bias, noise, cut_slopes, cut_heights, active_counts
):
    n = lax.axis_size("cuts")
    steps = early_steps(n)
    trials = trial_states[0]
    rows, width = trials.shape
    half, cuts = rows * n, cut_slopes.shape[0]

    other, other_ids = swap(trials, steps[0]), swap(scenario_ids, steps[0])
    scenarios = noise.shape[0]
    heights = cut_heights.reshape(cuts // LANES, LANES)
    sources = (trials, scenario_ids, dispatch, bias[None, :], noise, heights, cut_slopes)
    own, dispatch, bias, noise3, heights, slopes = pl.pallas_call(
        stage_kernel,
        out_shape=(
            jax.ShapeDtypeStruct((rows, width), jnp.bfloat16),
            jax.ShapeDtypeStruct(dispatch.shape, dispatch.dtype),
            jax.ShapeDtypeStruct((1, width), jnp.float32),
            jax.ShapeDtypeStruct((3 * scenarios, width), jnp.bfloat16),
            jax.ShapeDtypeStruct((cuts, LANES), jnp.float32),
            jax.ShapeDtypeStruct(cut_slopes.shape, cut_slopes.dtype),
        ),
        in_specs=[HBM] * 7,
        out_specs=(VMEM,) * 6,
        scratch_shapes=[
            pltpu.VMEM((rows, width), jnp.bfloat16),
            pltpu.VMEM(scenario_ids.shape, jnp.int32),
            pltpu.VMEM(noise.shape, jnp.float32),
            pltpu.VMEM((cuts // LANES, LANES), jnp.float32),
            pltpu.SemaphoreType.DMA((7,)),
        ],
        compiler_params=pltpu.CompilerParams(vmem_limit_bytes=16 * MIB),
        cost_estimate=pl.CostEstimate(
            flops=2 * rows * width * width,
            bytes_accessed=2 * width * (width + cuts),
            transcendentals=0,
        ),
        name="stage",
    )(*(pltpu.with_memory_space_constraint(array, pltpu.HBM) for array in sources))
    flow = pl.pallas_call(
        flow_kernel,
        out_shape=jax.ShapeDtypeStruct((rows, width), jnp.float32),
        in_specs=[VMEM] * 3,
        out_specs=VMEM,
        compiler_params=pltpu.CompilerParams(vmem_limit_bytes=8 * MIB),
        cost_estimate=pl.CostEstimate(
            flops=2 * rows * width * width, bytes_accessed=2 * width * width, transcendentals=0
        ),
        name="flow",
    )(other, dispatch, bias)
    held = pl.pallas_call(
        join_kernel,
        out_shape=jax.ShapeDtypeStruct((2 * rows, width), jnp.bfloat16),
        in_specs=[VMEM] * 4,
        out_specs=VMEM,
        compiler_params=pltpu.CompilerParams(vmem_limit_bytes=8 * MIB),
        cost_estimate=pl.CostEstimate(
            flops=6 * rows * scenarios * width, bytes_accessed=8 * rows * width, transcendentals=0
        ),
        name="inflow_join",
    )(own, flow, other_ids, noise3)
    offsets = [0, steps[0]]
    for step in steps[1:]:
        held = jnp.concatenate([held, swap(held, step)], axis=0)
        offsets = offsets + [offset ^ step for offset in offsets]
    pieces = [held] + [swap(held, step) for step in NEAR_STATES]
    offsets = [offset ^ step for step in (0, *NEAR_STATES) for offset in offsets]

    values, tops = pl.pallas_call(
        functools.partial(values_kernel, offsets, min(256, half)),
        out_shape=(
            jax.ShapeDtypeStruct((cuts, half), jnp.float32),
            jax.ShapeDtypeStruct((2, half), jnp.float32),
        ),
        in_specs=[SMEM] + [VMEM] * (2 + len(pieces)),
        out_specs=(VMEM, VMEM),
        scratch_shapes=[pltpu.VMEM((half, width), jnp.bfloat16)],
        compiler_params=pltpu.CompilerParams(vmem_limit_bytes=32 * MIB),
        cost_estimate=pl.CostEstimate(
            flops=2 * cuts * half * width, bytes_accessed=2 * cuts * width, transcendentals=0
        ),
        name="cut_values",
    )(active_counts, slopes, heights, *pieces)

    for step in steps[:-1]:
        tops = merge(tops, swap(tops, step))
    far = steps[-1]
    sets = [swap(tops, far * bit ^ near) for bit, near in ((1, 0), *EARLY_TOPS)]
    tops = merge(tops, sets[0])
    sets = [tops, *sets[1:], *(swap(tops, step) for step in LATE_TOPS)]

    chunk = min(256, cuts)
    return pl.pallas_call(
        functools.partial(margins_kernel, chunk),
        out_shape=jax.ShapeDtypeStruct((cuts, half), jnp.bfloat16),
        in_specs=[SMEM] + [VMEM] * (1 + len(sets)),
        out_specs=pl.BlockSpec(memory_space=pl.ANY),
        scratch_shapes=[
            pltpu.VMEM((cuts, half), jnp.bfloat16),
            pltpu.SemaphoreType.DMA((cuts // chunk,)),
        ],
        compiler_params=pltpu.CompilerParams(vmem_limit_bytes=16 * MIB),
        cost_estimate=pl.CostEstimate(
            flops=4 * cuts * half, bytes_accessed=2 * cuts * half, transcendentals=0
        ),
        name="margins",
    )(active_counts, values, *sets)


def solution(mesh):
    placed = (
        P("states", ("groups", "cuts"), None),
        P("states", ("groups", "cuts")),
        P(),
        P(),
        P("groups", None),
        P(("groups", "cuts"), None),
        P(("groups", "cuts")),
        P(("groups", "cuts")),
    )
    return jax.shard_map(
        on_device,
        mesh=mesh,
        in_specs=placed,
        out_specs=P(("groups", "cuts"), "states"),
        check_vma=False,
    )
```

```python
import functools

import jax
import jax.numpy as jnp
from jax import lax
from jax.experimental import pallas as pl
from jax.experimental.pallas import tpu as pltpu
from jax.sharding import PartitionSpec as P

NEG = -1e30
MIB = 1024 * 1024
LANES = 128
NEAR_STATES = (3, 1, 2)
EARLY_TOPS, LATE_TOPS = ((0, 1), (1, 1)), (3, 2)
VMEM = pl.BlockSpec(memory_space=pltpu.VMEM)
HBM = pl.BlockSpec(memory_space=pltpu.HBM)
SMEM = pl.BlockSpec(memory_space=pltpu.SMEM)


def swap(array, step):
    n = lax.axis_size("cuts")
    return lax.ppermute(array, "cuts", [(i, i ^ step) for i in range(n)])


def cross(array, step):
    n = lax.axis_size("cuts")
    pairs = [(2 * i + core, 2 * (i ^ step) + 1 - core) for i in range(n) for core in range(2)]
    return lax.ppermute(array, ("cuts", "states"), pairs)


def early_steps(n):
    steps, step = [], n // 2
    while step >= 4:
        steps.append(step)
        step //= 2
    return steps


def merge(left, right):
    high, low = jnp.maximum(left[0:1], right[0:1]), jnp.minimum(left[0:1], right[0:1])
    return jnp.concatenate([high, jnp.maximum(low, jnp.maximum(left[1:2], right[1:2]))], axis=0)


def split_in_three(values):
    high = values.astype(jnp.bfloat16)
    rest = values - high.astype(jnp.float32)
    mid = rest.astype(jnp.bfloat16)
    return high, mid, (rest - mid.astype(jnp.float32)).astype(jnp.bfloat16)


def inflow_of(ids, noise_ref):
    scenarios = lax.broadcasted_iota(jnp.int32, (noise_ref.shape[0] // 3, ids.shape[1]), 0)
    chosen = jnp.where(scenarios == ids, 1.0, 0.0)
    chosen = jnp.concatenate([chosen] * 3, axis=0).astype(jnp.bfloat16)
    return lax.dot_general(
        chosen, noise_ref[...], (((0,), (0,)), ((), ())), preferred_element_type=jnp.float32
    )


def flow_of(trials, dispatch_ref, bias):
    return jnp.dot(trials, dispatch_ref[...], preferred_element_type=jnp.float32) + bias


def next_of(flow, inflow):
    return jnp.maximum(flow + inflow, 0.0).astype(jnp.bfloat16)


def stage_kernel(
    trials_hbm, ids_hbm, dispatch_hbm, bias_hbm, noise_hbm, heights_hbm, slopes_hbm,
    own_ref, dispatch_ref, bias_ref, noise3_ref, columns_ref, slopes_ref,
    trials_ref, ids_ref, noise_ref, heights_ref, sems,
):
    pairs = (
        (noise_hbm, noise_ref),
        (trials_hbm, trials_ref),
        (ids_hbm, ids_ref),
        (bias_hbm, bias_ref),
        (heights_hbm, heights_ref),
        (dispatch_hbm, dispatch_ref),
        (slopes_hbm, slopes_ref),
    )
    copies = [pltpu.make_async_copy(src, dst, sems.at[i]) for i, (src, dst) in enumerate(pairs)]
    for copy in copies:
        copy.start()
    copies[0].wait()
    scenarios = noise_ref.shape[0]
    for i, term in enumerate(split_in_three(noise_ref[...])):
        noise3_ref[i * scenarios : (i + 1) * scenarios, :] = term
    for copy in copies[1:5]:
        copy.wait()
    for i in range(heights_ref.shape[0]):
        column = jnp.broadcast_to(heights_ref[i : i + 1, :], (LANES, LANES)).T
        columns_ref[i * LANES : (i + 1) * LANES, :] = column
    copies[5].wait()
    flow = flow_of(trials_ref[...], dispatch_ref, bias_ref[...])
    own_ref[...] = next_of(flow, inflow_of(ids_ref[...], noise3_ref))
    copies[6].wait()


def flow_kernel(other_ref, dispatch_ref, bias_ref, flow_ref):
    flow_ref[...] = flow_of(other_ref[...], dispatch_ref, bias_ref[...])


def join_kernel(own_ref, flow_ref, ids_ref, noise3_ref, out_ref):
    rows = own_ref.shape[0]
    out_ref[0:rows, :] = own_ref[...]
    out_ref[rows:, :] = next_of(flow_ref[...], inflow_of(ids_ref[...], noise3_ref))


def sublane_top_two(first, second):
    size = first.shape[0]
    while size > 1:
        half = size // 2
        a1, b1, a2, b2 = first[:half], first[half:size], second[:half], second[half:size]
        first, second = jnp.maximum(a1, b1), jnp.maximum(jnp.minimum(a1, b1), jnp.maximum(a2, b2))
        size = half
    return first, second


def values_kernel(offsets, block, *refs):
    counts_ref, slopes_ref, heights_ref = refs[:3]
    pieces, (values_ref, tops_ref, states_ref) = refs[3:-3], refs[-3:]
    me = lax.axis_index("cuts")
    held = len(offsets) // len(pieces)
    rows = pieces[0].shape[0] // held
    for i, offset in enumerate(offsets):
        piece, slot = pieces[i // held], i % held
        start = pl.multiple_of((me ^ offset) * rows, rows)
        states_ref[pl.ds(start, rows), :] = piece[slot * rows : (slot + 1) * rows, :]
    cuts, chunk = slopes_ref.shape[0], min(256, slopes_ref.shape[0])

    def on_block(column):
        states = states_ref[pl.ds(column, block), :]
        first = jnp.full((8, block), NEG, jnp.float32)
        second = first
        for start in range(0, cuts, chunk):
            here = lax.dot_general(
                slopes_ref[start : start + chunk, :],
                states,
                (((1,), (1,)), ((), ())),
                preferred_element_type=jnp.float32,
            )
            row = lax.broadcasted_iota(jnp.int32, (chunk, LANES), 0) + start
            heights = jnp.where(row < counts_ref[0], heights_ref[start : start + chunk, :], NEG)
            here = here + jnp.concatenate([heights] * (block // LANES), axis=1)
            values_ref[start : start + chunk, pl.ds(column, block)] = here
            for sub in range(0, chunk, 8):
                v = here[sub : sub + 8]
                second = jnp.maximum(second, jnp.minimum(first, v))
                first = jnp.maximum(first, v)
        first, second = sublane_top_two(first, second)
        tops_ref[0:1, pl.ds(column, block)] = first
        tops_ref[1:2, pl.ds(column, block)] = second

    blocks = states_ref.shape[0] // block
    if blocks == 1:
        on_block(0)
    else:

        @pl.loop(0, blocks)
        def _(b):
            on_block(pl.multiple_of(b * block, block))


def margins_kernel(chunk, counts_ref, values_ref, *refs):
    tops, (out_ref, held_ref, sems) = refs[:-3], refs[-3:]
    total = tops[0][...]
    for other in tops[1:]:
        total = merge(total, other[...])
    top1, top2 = total[0:1], total[1:2]
    count = counts_ref[0]
    cuts = values_ref.shape[0]
    copies = []
    for i in range(cuts // chunk):
        rows = slice(i * chunk, (i + 1) * chunk)
        values = values_ref[rows, :]
        row = lax.broadcasted_iota(jnp.int32, values.shape, 0) + i * chunk
        margin = values - jnp.where(values >= top1, top2, top1)
        held_ref[rows, :] = jnp.where(row < count, margin, 0.0).astype(jnp.bfloat16)
        copy = pltpu.make_async_copy(held_ref.at[rows], out_ref.at[rows], sems.at[i])
        copy.start()
        copies.append(copy)
    for copy in copies:
        copy.wait()


def on_device(
    trial_states, scenario_ids, dispatch, bias, noise, cut_slopes, cut_heights, active_counts
):
    n = lax.axis_size("cuts")
    steps = early_steps(n)
    trials = trial_states[0]
    rows, width = trials.shape
    half, cuts = rows * n, cut_slopes.shape[0]

    other, other_ids = swap(trials, steps[0]), swap(scenario_ids, steps[0])
    scenarios = noise.shape[0]
    heights = cut_heights.reshape(cuts // LANES, LANES)
    sources = (trials, scenario_ids, dispatch, bias[None, :], noise, heights, cut_slopes)
    own, dispatch, bias, noise3, heights, slopes = pl.pallas_call(
        stage_kernel,
        out_shape=(
            jax.ShapeDtypeStruct((rows, width), jnp.bfloat16),
            jax.ShapeDtypeStruct(dispatch.shape, dispatch.dtype),
            jax.ShapeDtypeStruct((1, width), jnp.float32),
            jax.ShapeDtypeStruct((3 * scenarios, width), jnp.bfloat16),
            jax.ShapeDtypeStruct((cuts, LANES), jnp.float32),
            jax.ShapeDtypeStruct(cut_slopes.shape, cut_slopes.dtype),
        ),
        in_specs=[HBM] * 7,
        out_specs=(VMEM,) * 6,
        scratch_shapes=[
            pltpu.VMEM((rows, width), jnp.bfloat16),
            pltpu.VMEM(scenario_ids.shape, jnp.int32),
            pltpu.VMEM(noise.shape, jnp.float32),
            pltpu.VMEM((cuts // LANES, LANES), jnp.float32),
            pltpu.SemaphoreType.DMA((7,)),
        ],
        compiler_params=pltpu.CompilerParams(vmem_limit_bytes=16 * MIB),
        cost_estimate=pl.CostEstimate(
            flops=2 * rows * width * width,
            bytes_accessed=2 * width * (width + cuts),
            transcendentals=0,
        ),
        name="stage",
    )(*(pltpu.with_memory_space_constraint(array, pltpu.HBM) for array in sources))
    flow = pl.pallas_call(
        flow_kernel,
        out_shape=jax.ShapeDtypeStruct((rows, width), jnp.float32),
        in_specs=[VMEM] * 3,
        out_specs=VMEM,
        compiler_params=pltpu.CompilerParams(vmem_limit_bytes=8 * MIB),
        cost_estimate=pl.CostEstimate(
            flops=2 * rows * width * width, bytes_accessed=2 * width * width, transcendentals=0
        ),
        name="flow",
    )(other, dispatch, bias)
    held = pl.pallas_call(
        join_kernel,
        out_shape=jax.ShapeDtypeStruct((2 * rows, width), jnp.bfloat16),
        in_specs=[VMEM] * 4,
        out_specs=VMEM,
        compiler_params=pltpu.CompilerParams(vmem_limit_bytes=8 * MIB),
        cost_estimate=pl.CostEstimate(
            flops=6 * rows * scenarios * width, bytes_accessed=8 * rows * width, transcendentals=0
        ),
        name="inflow_join",
    )(own, flow, other_ids, noise3)
    offsets = [0, steps[0]]
    for step in steps[1:]:
        held = jnp.concatenate([held, swap(held, step)], axis=0)
        offsets = offsets + [offset ^ step for offset in offsets]
    pieces = [held] + [swap(held, step) for step in NEAR_STATES]
    offsets = [offset ^ step for step in (0, *NEAR_STATES) for offset in offsets]

    values, tops = pl.pallas_call(
        functools.partial(values_kernel, offsets, min(256, half)),
        out_shape=(
            jax.ShapeDtypeStruct((cuts, half), jnp.float32),
            jax.ShapeDtypeStruct((2, half), jnp.float32),
        ),
        in_specs=[SMEM] + [VMEM] * (2 + len(pieces)),
        out_specs=(VMEM, VMEM),
        scratch_shapes=[pltpu.VMEM((half, width), jnp.bfloat16)],
        compiler_params=pltpu.CompilerParams(vmem_limit_bytes=32 * MIB),
        cost_estimate=pl.CostEstimate(
            flops=2 * cuts * half * width, bytes_accessed=2 * cuts * width, transcendentals=0
        ),
        name="cut_values",
    )(active_counts, slopes, heights, *pieces)

    for step in steps[:-1]:
        tops = merge(tops, swap(tops, step))
    far = steps[-1]
    mirror, met = cross(tops, 0), cross(tops, far)
    early = [swap(tops, far * bit ^ near) for bit, near in EARLY_TOPS]
    merged = merge(mirror, met)
    sets = [cross(merged, 0), *early, *(cross(merged, step) for step in LATE_TOPS)]

    chunk = min(256, cuts)
    return pl.pallas_call(
        functools.partial(margins_kernel, chunk),
        out_shape=jax.ShapeDtypeStruct((cuts, half), jnp.bfloat16),
        in_specs=[SMEM] + [VMEM] * (1 + len(sets)),
        out_specs=pl.BlockSpec(memory_space=pl.ANY),
        scratch_shapes=[
            pltpu.VMEM((cuts, half), jnp.bfloat16),
            pltpu.SemaphoreType.DMA((cuts // chunk,)),
        ],
        compiler_params=pltpu.CompilerParams(vmem_limit_bytes=16 * MIB),
        cost_estimate=pl.CostEstimate(
            flops=4 * cuts * half, bytes_accessed=2 * cuts * half, transcendentals=0
        ),
        name="margins",
    )(active_counts, values, *sets)


def solution(mesh):
    placed = (
        P("states", ("groups", "cuts"), None),
        P("states", ("groups", "cuts")),
        P(),
        P(),
        P("groups", None),
        P(("groups", "cuts"), None),
        P(("groups", "cuts")),
        P(("groups", "cuts")),
    )
    return jax.shard_map(
        on_device,
        mesh=mesh,
        in_specs=placed,
        out_specs=P(("groups", "cuts"), "states"),
        check_vma=False,
    )
```
